32 devices in a mesh: area: 4 (over z), dev: 8 (over y, x, core).
Axes of the slice: x: 2, y: 2, z: 4, core: 2. Of those that a mesh axis runs over, the one named last changes fastest.
Arguments:
- wave_fwd: float32 [3, 16384, 128], P(None, ('area', 'dev')), may hold values from -6 to 6
- wave_bwd: float32 [3, 16384, 128], P(None, ('area', 'dev')), may hold values from -6 to 6
- seg_reflect: float32 [3, 16384], P(None, ('area', 'dev')), may hold values from 0.04 to 0.4
- seg_count: int32 [32, 64], P(('area', 'dev')), may hold values from 1 to 24, 512 in all within a row
- modal_admit: float32 [3, 2048], P(None, ('area', 'dev')), may hold values from 0.02 to 0.2
- modal_transform: float32 [3, 3], replicated, may hold values from -3.5 to 3.5
- end_slot: int32 [2048, 2], P(('area', 'dev')), may hold values from 0 to 255, as said below
- recv_bus: int32 [32, 256], P(('area', 'dev')), may hold values from -1 to 63, as said below
- bus_impedance: float32 [3, 3, 2048], P(None, None, ('area', 'dev')), as said below
- link_bus: int32 [192, 2], P('area'), may hold values from 0 to 511, as said below
- link_resist: float32 [192], P('area'), may hold values from 0.5 to 5
- source_current: float32 [4, 2048, 3, 128], P(None, ('area', 'dev')), may hold values from -6 to 6
Outputs:
- bus_voltage: float32 [4, 2048, 3, 128], P(None, ('area', 'dev'))
- final_fwd: float32 [3, 16384, 128], P(None, ('area', 'dev'))
- final_bwd: float32 [3, 16384, 128], P(None, ('area', 'dev'))
The draws below stay inside these ranges and needn't reach their ends.
Inputs may be any that keep to these rules, and one draw needn't show every extreme that they name: `end_slot`: entry [l, s] is the slot of end s (0 sending, 1 receiving) of line l within its device's 32 blocks of 8 slots, block q // 8 going to owner device q // 8. The slots of one device are distinct. Every device fills all 8 slots of the block for some owner, and one owner receives 8 ends from every device. `recv_bus`: row r, column s * 8 + c: the local bus of device r to which slot c of device s's block for r attaches, and -1 exactly where no end of device s holds that slot. `link_bus`: the two buses of a link differ. `bus_impedance`: each bus's 3x3 matrix is symmetric with a positive diagonal larger than the sum of its row's other magnitudes.
All inputs are finite; a program needn't handle non-finite values.
Results may differ from the reference program's by a relative error of at most 0.00012.
Values sent between devices are 32-bit elements; how exact they have to be, the bound alone decides.
A program may use at most 64 MiB of HBM per device.

```python
import math
import jax
import jax.numpy as jnp
import numpy as np
from jax import lax

CASES = 128
STEPS = 4
SMAX = 24
LINES_DEV = 64
BUS_DEV = 64
LINK_AREA = 48
SEG_DEV = 512
CAP = 8
BUS_AREA = 512
LINES = 2048
SEGMENTS = 16384
BUSES = 2048
LINKS = 192
N_AREA = 4
DEVICES = 32


def routing_tables(key):
    base = jax.random.fold_in(key, 911)
    key_recv, key_own, key_slots, key_ends, key_bus = jax.random.split(base, 5)
    place_overall_sum = DEVICES * CAP
    every_holder_lookup = jax.random.randint(key_recv, (), 0, DEVICES)
    other = jax.random.randint(key_own, (DEVICES,), 0, DEVICES - 1)
    resident_holder_indicator = jnp.where(other >= every_holder_lookup, other + 1, other)
    place_holder_region = jnp.arange(place_overall_sum, dtype=jnp.int32) // CAP
    ordered_index_list = jax.vmap(lambda sub: jax.random.permutation(sub, place_overall_sum))(jax.random.split(key_slots, DEVICES))
    holder_preference_weight = 2 * (place_holder_region[None, :] == every_holder_lookup).astype(jnp.int32) + (place_holder_region[None, :] == resident_holder_indicator[:, None]).astype(jnp.int32)
    ordered_candidate_items = ordered_index_list.astype(jnp.int32) + place_overall_sum * holder_preference_weight
    top_values, chosen = lax.top_k(ordered_candidate_items, 2 * LINES_DEV)
    shuffle = jax.vmap(lambda sub: jax.random.permutation(sub, 2 * LINES_DEV))(jax.random.split(key_ends, DEVICES))
    picked = jnp.take_along_axis(chosen, shuffle, axis=1)
    rows = jnp.arange(DEVICES, dtype=jnp.int32)[:, None]
    used = jnp.zeros((DEVICES, place_overall_sum), jnp.int32).at[rows, chosen].set(1)
    used = used.reshape(DEVICES, DEVICES, CAP).transpose(1, 0, 2).reshape(DEVICES, place_overall_sum)
    buses = jax.random.randint(key_bus, (DEVICES, place_overall_sum), 0, BUS_DEV)
    received = jnp.where(used == 1, buses, -1)
    return (picked.reshape(DEVICES * LINES_DEV, 2).astype(jnp.int32), received.astype(jnp.int32))


def draw_end_slot(key, part):
    return routing_tables(key)[0]


def draw_recv_bus(key, part):
    return routing_tables(key)[1]


def draw_bus_impedance(key, part):
    key_diag, key_off = jax.random.split(jax.random.fold_in(key, 37), 2)
    diagonal = jax.random.uniform(key_diag, (3, BUSES), jnp.float32, 1.0, 2.0)
    raw = jax.random.uniform(key_off, (3, 3, BUSES), jnp.float32, -0.3, 0.3)
    symmetric = 0.5 * (raw + jnp.transpose(raw, (1, 0, 2)))
    identity = jnp.eye(3, dtype=jnp.float32)[:, :, None]
    matrix = identity * diagonal[None, :, :] + (1.0 - identity) * symmetric
    return matrix.astype(jnp.float32)


def draw_link_bus(key, part):
    key_from, key_gap = jax.random.split(jax.random.fold_in(key, 53), 2)
    start = jax.random.randint(key_from, (LINKS,), 0, BUS_AREA)
    gap = jax.random.randint(key_gap, (LINKS,), 1, BUS_AREA)
    finish = (start + gap) % BUS_AREA
    return jnp.stack([start, finish], axis=1).astype(jnp.int32)


def levels(rng, extent, cuts, least, top_value):
    gain = 1.0
    for dim, parts in cuts:
        draws = jax.random.uniform(jax.random.fold_in(jax.random.fold_in(rng, 6), dim), (parts,), jnp.float32, least / len(cuts), top_value / len(cuts))
        gain = gain * jnp.repeat(jnp.exp(draws), extent[dim] // parts).reshape((-1,) + (1,) * (len(extent) - 1 - dim))
    return gain


def split_up(number_of, total, bound, slope):
    weights = [(1 << 20) // math.isqrt(grade ** slope) + 1 for grade in range(2, number_of + 1)]
    surplus, given = total - bound - (number_of - 1), [1] * (number_of - 1)
    while surplus > 0:
        movable = [i for i in range(number_of - 1) if given[i] < bound]
        pool, budget = sum([weights[i] for i in movable]), surplus
        for i in movable:
            extra = min(bound - given[i], max(1, budget * weights[i] // pool), surplus)
            given[i] = given[i] + extra
            surplus = surplus - extra
    return np.array([bound] + given)


def ragged(rng, count, total, reach, lean):
    if count == 2:
        one = jax.random.randint(rng, (), max(1, total - reach), min(reach, total - 1) + 1)
        return jnp.stack([one, total - one])
    sizes = jnp.asarray(split_up(count, total, reach, lean), jnp.int32)
    pairs = (count - 1) // 2
    donor, receiver = sizes[1:1 + 2 * pairs:2], sizes[2:2 + 2 * pairs:2]
    slack = jnp.minimum(donor - 1, reach - receiver)
    moved = jax.random.randint(jax.random.fold_in(rng, 1), (pairs,), 0, 1 << 20) % (slack + 1)
    sizes = sizes.at[1:1 + 2 * pairs:2].set(donor - moved).at[2:2 + 2 * pairs:2].set(receiver + moved)
    return sizes[jax.random.permutation(jax.random.fold_in(rng, 2), count)]


def normal_values(key, shape, spread, bound, cuts=(), kind=jnp.bfloat16):
    drawn = jax.random.normal(key, shape, jnp.float32) * spread
    if len(cuts) > 0:
        drawn = levels(key, shape, cuts, -0.22, 0.18) * drawn
    return jnp.clip(drawn, min=-bound, max=bound).astype(kind)


def setup_inputs(seed: int = 0) -> dict:
    streams_of = jax.random.split(jax.random.key(seed), 13)
    wave_fwd = normal_values(streams_of[0], (3, SEGMENTS, CASES), 1.0, 6.0, ((1, 32),), jnp.float32)
    wave_bwd = normal_values(streams_of[1], (3, SEGMENTS, CASES), 1.0, 6.0, ((1, 32),), jnp.float32)
    seg_reflect = jnp.clip(jnp.exp(math.log(0.4) - 2.3025851 * jax.random.uniform(streams_of[2], (3, SEGMENTS), jnp.float32) ** levels(streams_of[2], (3, SEGMENTS), ((1, 32),), -0.2, 0.2)), 0.04, 0.4)
    seg_count = jax.vmap(lambda own: ragged(own, LINES_DEV, SEG_DEV, SMAX, 2))(jax.random.split(streams_of[3], DEVICES)).reshape((DEVICES, LINES_DEV)).astype(jnp.int32)
    modal_admit = jnp.clip(jnp.exp(math.log(0.2) - 2.3025851 * jax.random.uniform(streams_of[4], (3, LINES), jnp.float32) ** levels(streams_of[4], (3, LINES), ((1, 32),), -0.2, 0.2)), 0.02, 0.2)
    modal_transform = normal_values(streams_of[5], (3, 3), 3 ** -0.5, 3.5, (), jnp.float32)
    end_slot = draw_end_slot(jax.random.fold_in(streams_of[12], 71), 0)
    recv_bus = draw_recv_bus(jax.random.fold_in(streams_of[12], 71), 0)
    bus_impedance = draw_bus_impedance(jax.random.fold_in(streams_of[12], 71), 0)
    link_bus = draw_link_bus(jax.random.fold_in(streams_of[12], 71), 0)
    link_resist = jnp.clip(jnp.exp(math.log(5.0) - 2.3025851 * jax.random.uniform(streams_of[10], (LINKS,), jnp.float32) ** levels(streams_of[10], (LINKS,), ((0, 4),), -0.2, 0.2)), 0.5, 5.0)
    source_current = normal_values(streams_of[11], (STEPS, BUSES, 3, CASES), 1.0, 6.0, ((1, 32),), jnp.float32)
    return dict(wave_fwd=wave_fwd, wave_bwd=wave_bwd, seg_reflect=seg_reflect, seg_count=seg_count, modal_admit=modal_admit, modal_transform=modal_transform, end_slot=end_slot, recv_bus=recv_bus, bus_impedance=bus_impedance, link_bus=link_bus, link_resist=link_resist, source_current=source_current)


def solve_links(factor, rhs):
    lower = lax.linalg.triangular_solve(factor, rhs, left_side=True, lower=True)
    return lax.linalg.triangular_solve(factor, lower, left_side=True, lower=True, transpose_a=True)

def reference(wave_fwd, wave_bwd, seg_reflect, seg_count, modal_admit, modal_transform, end_slot, recv_bus, bus_impedance, link_bus, link_resist, source_current):
    exact = lax.Precision.HIGHEST
    counts = seg_count.astype(jnp.int32)
    local_first = (jnp.cumsum(counts, axis=1) - counts).astype(jnp.int32)
    offsets = (jnp.arange(DEVICES, dtype=jnp.int32) * SEG_DEV)[:, None]
    first = (local_first + offsets).reshape(-1).astype(jnp.int32)
    last = (first + counts.reshape(-1) - 1).astype(jnp.int32)
    line_device = (jnp.arange(LINES, dtype=jnp.int32) // LINES_DEV)[:, None]
    owner = (end_slot // CAP).astype(jnp.int32)
    column = (line_device * CAP + end_slot % CAP).astype(jnp.int32)
    end_bus = (owner * BUS_DEV + recv_bus[owner, column]).reshape(-1).astype(jnp.int32)
    bus_index = jnp.arange(BUS_AREA, dtype=jnp.int32)
    incidences = []
    factors = []
    for area in range(N_AREA):
        links = link_bus[area * LINK_AREA:(area + 1) * LINK_AREA]
        incidence = (bus_index[:, None] == links[None, :, 0]).astype(jnp.float32) - (bus_index[:, None] == links[None, :, 1]).astype(jnp.float32)
        imped = bus_impedance[:, :, area * BUS_AREA:(area + 1) * BUS_AREA]
        matrix = jnp.einsum('bl,ijb,bm->limj', incidence, imped, incidence, precision=exact).reshape(3 * LINK_AREA, 3 * LINK_AREA)
        matrix = matrix + jnp.diag(jnp.repeat(link_resist[area * LINK_AREA:(area + 1) * LINK_AREA], 3))
        incidences.append(incidence)
        factors.append(jnp.linalg.cholesky(matrix))
    forward, backward = (wave_fwd, wave_bwd)
    reflect = seg_reflect
    reflect_next = jnp.roll(seg_reflect, -1, axis=1)
    voltages = []
    for step in range(STEPS):
        arriving = jnp.stack([backward[:, first, :], forward[:, last, :]], axis=2)
        history = 2.0 * jnp.einsum('mi,mlsk->lsik', modal_transform, modal_admit[:, :, None, None] * arriving, precision=exact)
        summed = jax.ops.segment_sum(history.reshape(2 * LINES, 3, CASES), end_bus, num_segments=BUSES)
        inject = source_current[step] + summed
        open_volts = jnp.einsum('ijb,bjk->bik', bus_impedance, inject, precision=exact)
        pieces = []
        for area in range(N_AREA):
            rows = slice(area * BUS_AREA, (area + 1) * BUS_AREA)
            sources = jnp.einsum('bl,bik->lik', incidences[area], open_volts[rows], precision=exact).reshape(3 * LINK_AREA, CASES)
            current = solve_links(factors[area], sources).reshape(LINK_AREA, 3, CASES)
            pieces.append(inject[rows] - jnp.einsum('bl,lik->bik', incidences[area], current, precision=exact))
        volts = jnp.einsum('ijb,bjk->bik', bus_impedance, jnp.concatenate(pieces, axis=0), precision=exact)
        voltages.append(volts)
        end_volts = volts[end_bus].reshape(LINES, 2, 3, CASES)
        outgoing = jnp.einsum('mi,lsik->mlsk', modal_transform, end_volts, precision=exact) - arriving
        fwd_next = (1.0 - reflect)[:, :, None] * jnp.roll(forward, 1, axis=1) + reflect[:, :, None] * backward
        fwd_next = fwd_next.at[:, first, :].set(outgoing[:, :, 0, :])
        bwd_next = (1.0 - reflect_next)[:, :, None] * jnp.roll(backward, -1, axis=1) + reflect_next[:, :, None] * forward
        bwd_next = bwd_next.at[:, last, :].set(outgoing[:, :, 1, :])
        forward, backward = (fwd_next, bwd_next)
    return (jnp.stack(voltages), forward, backward)
```

```python
import functools

import jax
import jax.numpy as jnp
from jax import lax
from jax.experimental import pallas as pl
from jax.experimental.pallas import tpu as pltpu
from jax.sharding import PartitionSpec as P

STEPS = 4
MESH = pl.DeviceIdType.MESH
F32 = jnp.float32
BF16 = jnp.bfloat16
EXACT = lax.Precision.HIGHEST


def iota(shape, dim):
    return lax.broadcasted_iota(jnp.int32, shape, dim)


def to_column(row):
    n = row.shape[1]
    eye = iota((n, n), 0) == iota((n, n), 1)
    return jnp.sum(jnp.where(eye, row, 0.0), axis=1, keepdims=True)


def to_row(column):
    n = column.shape[0]
    eye = iota((n, n), 0) == iota((n, n), 1)
    return jnp.sum(jnp.where(eye, column, 0.0), axis=0, keepdims=True)


def onehot(flag):
    return jnp.where(flag, 1.0, 0.0).astype(BF16)


def pick(matrix, value):
    n = value.shape[1]
    high = value.astype(BF16)
    low = (value - high.astype(F32)).astype(BF16)
    both = jnp.dot(
        matrix, jnp.concatenate([high, low], axis=1), preferred_element_type=F32
    )
    return both[:, :n] + both[:, n:]


def kernel(
    areas,
    devs,
    link_real,
    fwd_in,
    bwd_in,
    refl_ref,
    count_ref,
    admit_ref,
    trans_ref,
    slot_ref,
    recv_ref,
    imp_ref,
    link_ref,
    resist_ref,
    src_ref,
    volt_ref,
    fwd,
    bwd,
    h_send,
    h_recv,
    e_send,
    e_recv,
    g_send,
    g_recv,
    v_send,
    v_recv,
    imp_all,
    gb,
    gf,
    gbt,
    gft,
    rsum,
    rback,
    ct,
    cm,
    adm,
    zcol,
    keep_f,
    take_f,
    keep_b,
    take_b,
    arr,
    inj,
    minv,
    send_sem,
    recv_sem,
    imp_sem,
):
    total = areas * devs
    area, dev = lax.axis_index("area"), lax.axis_index("dev")
    me = area * devs + dev
    cases = fwd.shape[2]
    segs = fwd.shape[1]
    lines = slot_ref.shape[0]
    slots = recv_ref.shape[1]
    buses = imp_ref.shape[1]
    links = link_ref.shape[0]
    cap = slots // total
    lp = links // devs

    barrier = pltpu.get_barrier_semaphore()

    def peer_of(p):
        peer = lax.rem(me + p, total)
        return peer, (peer // devs, lax.rem(peer, devs))

    @pl.loop(1, total)
    def _(p):
        _, where = peer_of(p)
        pl.semaphore_signal(barrier, inc=1, device_id=where, device_id_type=MESH)

    def push_all(send, recv, phase, step):
        @pl.loop(1, total)
        def _(p):
            peer, where = peer_of(p)
            pltpu.make_async_remote_copy(
                src_ref=send.at[step, peer],
                dst_ref=recv.at[step, me],
                send_sem=send_sem.at[phase, step],
                recv_sem=recv_sem.at[phase, step],
                device_id=where,
                device_id_type=MESH,
            ).start()

    def push_area(source, recv, phase, step):
        @pl.loop(1, devs)
        def _(p):
            other = lax.rem(dev + p, devs)
            pltpu.make_async_remote_copy(
                src_ref=source(other),
                dst_ref=recv.at[step, dev],
                send_sem=send_sem.at[phase, step],
                recv_sem=recv_sem.at[phase, step],
                device_id=(area, other),
                device_id_type=MESH,
            ).start()

    def wait(buf, count, sem):
        ref = buf.at[pl.ds(0, count)]
        pltpu.make_async_copy(ref, ref, sem).wait()

    counts_row = count_ref[...].astype(F32)
    counts_col = to_column(counts_row)
    square = (lines, lines)
    first_col = jnp.sum(
        jnp.where(iota(square, 1) < iota(square, 0), counts_row, 0.0), axis=1, keepdims=True
    )
    first_row = to_row(first_col)
    last_col = first_col + counts_col - 1.0
    last_row = first_row + counts_row - 1.0
    slot0_col = slot_ref[:, 0:1].astype(F32)
    slot1_col = slot_ref[:, 1:2].astype(F32)
    slot0_row, slot1_row = to_row(slot0_col), to_row(slot1_col)
    seg_lane = iota((lines, segs), 1).astype(F32)
    seg_sub = iota((segs, lines), 0).astype(F32)
    slot_lane = iota((lines, slots), 1).astype(F32)
    slot_sub = iota((slots, lines), 0).astype(F32)
    q0, q1 = onehot(slot_sub == slot0_row), onehot(slot_sub == slot1_row)
    gb[...] = jnp.dot(q0, onehot(seg_lane == first_col), preferred_element_type=F32).astype(BF16)
    gf[...] = jnp.dot(q1, onehot(seg_lane == last_col), preferred_element_type=F32).astype(BF16)
    held = q0.astype(F32) + q1.astype(F32)
    for m in range(3):
        column = 2.0 * jnp.sum(held * admit_ref[m : m + 1, :], axis=1, keepdims=True)
        adm[m] = jnp.broadcast_to(column, (slots, cases))

    def gather_send(step):
        for m in range(3):
            arr[m] = pick(gb[...], bwd[m]) + pick(gf[...], fwd[m])
        for i in range(3):
            value = trans_ref[0, i] * (adm[0] * arr[0])
            value = value + trans_ref[1, i] * (adm[1] * arr[1])
            value = value + trans_ref[2, i] * (adm[2] * arr[2])
            h_send[step, :, :, i * cases : (i + 1) * cases] = value.reshape(total, cap, cases)
        push_all(h_send, h_recv, 0, step)
        h_recv[step, me] = h_send[step, me]

    fwd[...] = fwd_in[...]
    bwd[...] = bwd_in[...]
    pl.semaphore_wait(barrier, total - 1)

    @pl.loop(1, devs)
    def _(p):
        other = lax.rem(dev + p, devs)
        pltpu.make_async_remote_copy(
            src_ref=imp_ref,
            dst_ref=imp_all.at[dev],
            send_sem=imp_sem.at[0],
            recv_sem=imp_sem.at[1],
            device_id=(area, other),
            device_id_type=MESH,
        ).start()

    gather_send(0)
    imp_all[dev] = imp_ref[...]

    fst = onehot(seg_sub == first_row)
    lst = onehot(seg_sub == last_row)
    gbt[...] = jnp.dot(fst, onehot(slot_lane == slot0_col), preferred_element_type=F32).astype(BF16)
    gft[...] = jnp.dot(lst, onehot(slot_lane == slot1_col), preferred_element_type=F32).astype(BF16)
    not_first = 1.0 - jnp.sum(fst.astype(F32), axis=1, keepdims=True)
    not_last = 1.0 - jnp.sum(lst.astype(F32), axis=1, keepdims=True)
    for m in range(3):
        r = to_column(refl_ref[m : m + 1, :])
        r_next = pltpu.roll(jnp.broadcast_to(r, (segs, cases)), segs - 1, 0)
        keep_f[m] = jnp.broadcast_to((1.0 - r) * not_first, (segs, cases))
        take_f[m] = jnp.broadcast_to(r * not_first, (segs, cases))
        keep_b[m] = (1.0 - r_next) * not_last
        take_b[m] = r_next * not_last
    recv_row = recv_ref[...].astype(F32)
    rsum[...] = onehot(iota((buses, slots), 0).astype(F32) == recv_row)
    rback[...] = onehot(iota((slots, buses), 1).astype(F32) == to_column(recv_row))
    link0, link1 = link_ref[:, 0:1].astype(F32), link_ref[:, 1:2].astype(F32)

    def incidence(d):
        index = (iota((links, buses), 1) + d * buses).astype(F32)
        return jnp.where(index == link0, 1.0, 0.0) - jnp.where(index == link1, 1.0, 0.0)

    ct[...] = incidence(dev).astype(BF16)
    index = (iota((buses, links), 0) + dev * buses).astype(F32)
    cm[...] = (
        jnp.where(index == to_row(link0), 1.0, 0.0) - jnp.where(index == to_row(link1), 1.0, 0.0)
    ).astype(BF16)
    for ij in range(9):
        zcol[ij] = jnp.broadcast_to(to_column(imp_ref[ij : ij + 1, :]), (buses, cases))

    def advance():
        for m in range(3):
            f, b = fwd[m], bwd[m]
            fwd[m] = keep_f[m] * pltpu.roll(f, 1, 0) + take_f[m] * b
            bwd[m] = keep_b[m] * pltpu.roll(b, segs - 1, 0) + take_b[m] * f

    wait(imp_all, devs - 1, imp_sem.at[1])
    minv[...] = jnp.zeros_like(minv)
    eye = iota((links, links), 0) == iota((links, links), 1)

    @pl.loop(0, devs)
    def _(d):
        c = incidence(d)
        for i in range(3):
            for j in range(3):
                z = imp_all[d, 3 * i + j : 3 * i + j + 1, :]
                minv[i * links : (i + 1) * links, j * links : (j + 1) * links] += lax.dot_general(
                    c * z, c, (((1,), (1,)), ((), ())), precision=EXACT, preferred_element_type=F32
                )

    for i in range(3):
        span = slice(i * links, (i + 1) * links)
        minv[span, span] += jnp.where(eye, resist_ref[...], 0.0)
    order = 3 * links
    lane, sub = iota((order, order), 1), iota((order, order), 0)

    @pl.loop(0, 3 * link_real * devs)
    def _(n):
        i, l = n // (link_real * devs), lax.rem(n, link_real * devs)
        k = i * links + (l // link_real) * lp + lax.rem(l, link_real)
        a = minv[...]
        row = minv[pl.ds(k, 1), :]
        here = lane == k
        col = jnp.sum(jnp.where(here, a, 0.0), axis=1, keepdims=True)
        pivot = jnp.sum(jnp.where(lane[:1] == k, row, 0.0), axis=1, keepdims=True)
        inverse = 1.0 / pivot
        scaled_row = row * inverse
        scaled_col = col * inverse
        rest = jnp.where(here, scaled_col, a - col * scaled_row)
        edge = jnp.where(lane[:1] == k, -inverse, scaled_row)
        minv[...] = jnp.where(sub == k, edge, rest)

    def apply(step, values):
        return [
            zcol[3 * i] * values[0] + zcol[3 * i + 1] * values[1] + zcol[3 * i + 2] * values[2]
            for i in range(3)
        ]

    def finish(step):
        advance()
        wait(h_recv.at[step], total - 1, recv_sem.at[0, step])
        for i in range(3):
            part = h_recv[step, :, :, i * cases : (i + 1) * cases].reshape(slots, cases)
            inj[i] = src_ref[step, :, i, :] + pick(rsum[...], part)
        open_volts = apply(step, [inj[i] for i in range(3)])
        for i in range(3):
            e_send[step, :, :, i * cases : (i + 1) * cases] = pick(
                ct[...], open_volts[i]
            ).reshape(devs, lp, cases)
        push_area(lambda other: e_send.at[step, other], e_recv, 1, step)
        e_recv[step, dev] = e_send[step, dev]
        wait(e_recv.at[step], devs - 1, recv_sem.at[1, step])
        g_send[step] = jnp.sum(e_recv[step], axis=0)
        push_area(lambda other: g_send.at[step], g_recv, 2, step)
        g_recv[step, dev] = g_send[step]
        wait(g_recv.at[step], devs - 1, recv_sem.at[2, step])
        stacked = jnp.concatenate(
            [
                g_recv[step, :, :, i * cases : (i + 1) * cases].reshape(links, cases)
                for i in range(3)
            ],
            axis=0,
        )
        current = jnp.dot(minv[...], stacked, precision=EXACT, preferred_element_type=F32)
        net = [
            inj[i] + pick(cm[...], current[i * links : (i + 1) * links]) for i in range(3)
        ]
        volts = apply(step, net)
        for i in range(3):
            volt_ref[step, :, i, :] = volts[i]
            v_send[step, :, :, i * cases : (i + 1) * cases] = pick(rback[...], volts[i]).reshape(
                total, cap, cases
            )
        push_all(v_send, v_recv, 3, step)
        v_recv[step, me] = v_send[step, me]
        wait(v_recv.at[step], total - 1, recv_sem.at[3, step])
        ends = [
            v_recv[step, :, :, i * cases : (i + 1) * cases].reshape(slots, cases) for i in range(3)
        ]
        for m in range(3):
            out = trans_ref[m, 0] * ends[0] + trans_ref[m, 1] * ends[1] + trans_ref[m, 2] * ends[2]
            out = out - arr[m]
            fwd[m] += pick(gbt[...], out)
            bwd[m] += pick(gft[...], out)

    finish(0)

    @pl.loop(1, STEPS)
    def _(step):
        gather_send(step)
        finish(step)

    wait(imp_all, devs - 1, imp_sem.at[0])

    @pl.loop(0, STEPS)
    def _(step):
        wait(h_send.at[step], total - 1, send_sem.at[0, step])
        wait(e_send.at[step], devs - 1, send_sem.at[1, step])
        wait(g_recv.at[step], devs - 1, send_sem.at[2, step])
        wait(v_send.at[step], total - 1, send_sem.at[3, step])


def on_device(
    areas,
    devs,
    wave_fwd,
    wave_bwd,
    seg_reflect,
    seg_count,
    modal_admit,
    modal_transform,
    end_slot,
    recv_bus,
    bus_impedance,
    link_bus,
    link_resist,
    source_current,
):
    total = areas * devs
    cases, segs = wave_fwd.shape[2], wave_fwd.shape[1]
    cap = recv_bus.shape[1] // total
    rows = -(-cap // 8) * 8
    if rows != cap:
        end_slot = end_slot // cap * rows + end_slot % cap
        recv_bus = jnp.pad(
            recv_bus.reshape(total, cap), ((0, 0), (0, rows - cap)), constant_values=-1
        ).reshape(1, total * rows)
    slots = total * rows
    buses = bus_impedance.shape[2]
    link_real = link_bus.shape[0] // devs
    lp = -(-link_real // 8) * 8
    links = lp * devs
    link_pad = jnp.pad(
        link_bus.reshape(devs, link_real, 2),
        ((0, 0), (0, lp - link_real), (0, 0)),
        constant_values=-1,
    ).reshape(links, 2)
    resist_pad = jnp.pad(
        link_resist.reshape(devs, link_real), ((0, 0), (0, lp - link_real)), constant_values=1.0
    ).reshape(links, 1)
    impedance = bus_impedance.reshape(9, buses)
    vmem = pl.BlockSpec(memory_space=pltpu.VMEM)
    smem = pl.BlockSpec(memory_space=pltpu.SMEM)
    wide = 3 * cases
    return pl.pallas_call(
        functools.partial(kernel, areas, devs, link_real),
        out_shape=(
            jax.ShapeDtypeStruct(source_current.shape, F32),
            jax.ShapeDtypeStruct(wave_fwd.shape, F32),
            jax.ShapeDtypeStruct(wave_bwd.shape, F32),
        ),
        in_specs=[vmem] * 5 + [smem] + [vmem] * 6,
        out_specs=(vmem, vmem, vmem),
        scratch_shapes=[
            pltpu.VMEM((STEPS, total, rows, wide), F32),
            pltpu.VMEM((STEPS, total, rows, wide), F32),
            pltpu.VMEM((STEPS, devs, lp, wide), F32),
            pltpu.VMEM((STEPS, devs, lp, wide), F32),
            pltpu.VMEM((STEPS, lp, wide), F32),
            pltpu.VMEM((STEPS, devs, lp, wide), F32),
            pltpu.VMEM((STEPS, total, rows, wide), F32),
            pltpu.VMEM((STEPS, total, rows, wide), F32),
            pltpu.VMEM((devs, 9, buses), F32),
            pltpu.VMEM((slots, segs), BF16),
            pltpu.VMEM((slots, segs), BF16),
            pltpu.VMEM((segs, slots), BF16),
            pltpu.VMEM((segs, slots), BF16),
            pltpu.VMEM((buses, slots), BF16),
            pltpu.VMEM((slots, buses), BF16),
            pltpu.VMEM((links, buses), BF16),
            pltpu.VMEM((buses, links), BF16),
            pltpu.VMEM((3, slots, cases), F32),
            pltpu.VMEM((9, buses, cases), F32),
            pltpu.VMEM((3, segs, cases), F32),
            pltpu.VMEM((3, segs, cases), F32),
            pltpu.VMEM((3, segs, cases), F32),
            pltpu.VMEM((3, segs, cases), F32),
            pltpu.VMEM((3, slots, cases), F32),
            pltpu.VMEM((3, buses, cases), F32),
            pltpu.VMEM((3 * links, 3 * links), F32),
            pltpu.SemaphoreType.DMA((4, STEPS)),
            pltpu.SemaphoreType.DMA((4, STEPS)),
            pltpu.SemaphoreType.DMA((2,)),
        ],
        compiler_params=pltpu.CompilerParams(
            collective_id=0, has_side_effects=True, vmem_limit_bytes=60 * 1024 * 1024
        ),
        name="transient",
    )(
        wave_fwd,
        wave_bwd,
        seg_reflect,
        seg_count,
        modal_admit,
        modal_transform,
        end_slot,
        recv_bus,
        impedance,
        link_pad,
        resist_pad,
        source_current,
    )


def solution(mesh):
    in_specs = (
        P(None, ("area", "dev"), None),
        P(None, ("area", "dev"), None),
        P(None, ("area", "dev")),
        P(("area", "dev"), None),
        P(None, ("area", "dev")),
        P(),
        P(("area", "dev"), None),
        P(("area", "dev"), None),
        P(None, None, ("area", "dev")),
        P("area", None),
        P("area"),
        P(None, ("area", "dev"), None, None),
    )
    out_specs = (
        P(None, ("area", "dev"), None, None),
        P(None, ("area", "dev"), None),
        P(None, ("area", "dev"), None),
    )
    return jax.shard_map(
        functools.partial(on_device, mesh.shape["area"], mesh.shape["dev"]),
        mesh=mesh,
        in_specs=in_specs,
        out_specs=out_specs,
        check_vma=False,
    )
```

```python
import functools

import jax
import jax.numpy as jnp
from jax import lax
from jax.experimental import pallas as pl
from jax.experimental.pallas import tpu as pltpu
from jax.sharding import PartitionSpec as P

STEPS = 4
MESH = pl.DeviceIdType.MESH
F32 = jnp.float32
BF16 = jnp.bfloat16
EXACT = lax.Precision.HIGHEST


def iota(shape, dim):
    return lax.broadcasted_iota(jnp.int32, shape, dim)


def to_column(row):
    n = row.shape[1]
    eye = iota((n, n), 0) == iota((n, n), 1)
    return jnp.sum(jnp.where(eye, row, 0.0), axis=1, keepdims=True)


def to_row(column):
    n = column.shape[0]
    eye = iota((n, n), 0) == iota((n, n), 1)
    return jnp.sum(jnp.where(eye, column, 0.0), axis=0, keepdims=True)


def onehot(flag):
    return jnp.where(flag, 1.0, 0.0).astype(BF16)


def pick(matrix, value):
    n = value.shape[1]
    high = value.astype(BF16)
    low = (value - high.astype(F32)).astype(BF16)
    both = jnp.dot(
        matrix, jnp.concatenate([high, low], axis=1), preferred_element_type=F32
    )
    return both[:, :n] + both[:, n:]


def kernel(
    areas,
    devs,
    fwd_in,
    bwd_in,
    refl_ref,
    count_ref,
    admit_ref,
    trans_ref,
    slot_ref,
    recv_ref,
    imp_ref,
    link_ref,
    resist_ref,
    src_ref,
    volt_ref,
    fwd,
    bwd,
    h_send,
    h_recv,
    e_send,
    e_recv,
    g_recv,
    v_send,
    v_recv,
    imp_all,
    gb,
    gf,
    gbt,
    gft,
    rsum,
    rback,
    ct,
    cm,
    adm,
    zcol,
    keep_f,
    take_f,
    keep_b,
    take_b,
    arr,
    inj,
    minv,
    send_sem,
    recv_sem,
    imp_sem,
):
    total = areas * devs
    area, dev = lax.axis_index("area"), lax.axis_index("dev")
    me = area * devs + dev
    cases = fwd.shape[2]
    segs = fwd.shape[1]
    lines = slot_ref.shape[1]
    slots = recv_ref.shape[1]
    buses = imp_ref.shape[2]
    links = link_ref.shape[1]
    owners = links // 8
    cap = slots // total

    barrier = pltpu.get_barrier_semaphore()

    def peer_of(p):
        peer = lax.rem(me + p, total)
        return peer, (peer // devs, lax.rem(peer, devs))

    @pl.loop(1, total)
    def _(p):
        _, where = peer_of(p)
        pl.semaphore_signal(barrier, inc=1, device_id=where, device_id_type=MESH)

    def push_all(send, recv, phase, step):
        @pl.loop(1, total)
        def _(p):
            peer, where = peer_of(p)
            pltpu.make_async_remote_copy(
                src_ref=send.at[step, peer],
                dst_ref=recv.at[step, me],
                send_sem=send_sem.at[phase, step],
                recv_sem=recv_sem.at[phase, step],
                device_id=where,
                device_id_type=MESH,
            ).start()

    def push_shares(step):
        @pl.loop(0, owners)
        def _(other):
            @pl.when(other != dev)
            def _():
                pltpu.make_async_remote_copy(
                    src_ref=e_send.at[step, other],
                    dst_ref=e_recv.at[step, dev],
                    send_sem=send_sem.at[1, step],
                    recv_sem=recv_sem.at[1, step],
                    device_id=(area, other),
                    device_id_type=MESH,
                ).start()

    def sum_shares(step):
        e_recv[step, dev] = e_send[step, dev]
        wait(e_recv.at[step], devs - 1, recv_sem.at[1, step])
        g_recv[step, dev] = jnp.sum(e_recv[step], axis=0)

        @pl.loop(1, devs)
        def _(p):
            other = lax.rem(dev + p, devs)
            pltpu.make_async_remote_copy(
                src_ref=g_recv.at[step, dev],
                dst_ref=g_recv.at[step, dev],
                send_sem=send_sem.at[2, step],
                recv_sem=recv_sem.at[2, step],
                device_id=(area, other),
                device_id_type=MESH,
            ).start()

    def wait(buf, count, sem):
        ref = buf.at[pl.ds(0, count)]
        pltpu.make_async_copy(ref, ref, sem).wait()

    counts_row = count_ref[...].astype(F32)
    counts_col = to_column(counts_row)
    square = (lines, lines)
    first_col = jnp.sum(
        jnp.where(iota(square, 1) < iota(square, 0), counts_row, 0.0), axis=1, keepdims=True
    )
    first_row = to_row(first_col)
    last_col = first_col + counts_col - 1.0
    last_row = first_row + counts_row - 1.0
    slot0_row = slot_ref[0:1, :].astype(F32)
    slot1_row = slot_ref[1:2, :].astype(F32)
    slot0_col, slot1_col = to_column(slot0_row), to_column(slot1_row)
    seg_lane = iota((lines, segs), 1).astype(F32)
    seg_sub = iota((segs, lines), 0).astype(F32)
    slot_lane = iota((lines, slots), 1).astype(F32)
    slot_sub = iota((slots, lines), 0).astype(F32)
    q0, q1 = onehot(slot_sub == slot0_row), onehot(slot_sub == slot1_row)
    gb[...] = jnp.dot(q0, onehot(seg_lane == first_col), preferred_element_type=F32).astype(BF16)
    gf[...] = jnp.dot(q1, onehot(seg_lane == last_col), preferred_element_type=F32).astype(BF16)
    held = q0.astype(F32) + q1.astype(F32)
    for m in range(3):
        column = 2.0 * jnp.sum(held * admit_ref[m : m + 1, :], axis=1, keepdims=True)
        adm[m] = jnp.broadcast_to(column, (slots, cases))

    def gather_send(step):
        for m in range(3):
            arr[m] = pick(gb[...], bwd[m]) + pick(gf[...], fwd[m])
        for i in range(3):
            value = trans_ref[0, i] * (adm[0] * arr[0])
            value = value + trans_ref[1, i] * (adm[1] * arr[1])
            value = value + trans_ref[2, i] * (adm[2] * arr[2])
            h_send[step, :, :, i * cases : (i + 1) * cases] = value.reshape(total, cap, cases)
        push_all(h_send, h_recv, 0, step)
        h_recv[step, me] = h_send[step, me]

    fwd[...] = fwd_in[...]
    bwd[...] = bwd_in[...]
    pl.semaphore_wait(barrier, total - 1)

    @pl.loop(1, devs)
    def _(p):
        other = lax.rem(dev + p, devs)
        pltpu.make_async_remote_copy(
            src_ref=imp_ref,
            dst_ref=imp_all.at[dev],
            send_sem=imp_sem.at[0],
            recv_sem=imp_sem.at[1],
            device_id=(area, other),
            device_id_type=MESH,
        ).start()

    gather_send(0)
    imp_all[dev] = imp_ref[...]

    fst = onehot(seg_sub == first_row)
    lst = onehot(seg_sub == last_row)
    gbt[...] = jnp.dot(fst, onehot(slot_lane == slot0_col), preferred_element_type=F32).astype(BF16)
    gft[...] = jnp.dot(lst, onehot(slot_lane == slot1_col), preferred_element_type=F32).astype(BF16)
    not_first = 1.0 - jnp.sum(fst.astype(F32), axis=1, keepdims=True)
    not_last = 1.0 - jnp.sum(lst.astype(F32), axis=1, keepdims=True)
    for m in range(3):
        r = to_column(refl_ref[m : m + 1, :])
        r_next = pltpu.roll(jnp.broadcast_to(r, (segs, cases)), segs - 1, 0)
        keep_f[m] = jnp.broadcast_to((1.0 - r) * not_first, (segs, cases))
        take_f[m] = jnp.broadcast_to(r * not_first, (segs, cases))
        keep_b[m] = (1.0 - r_next) * not_last
        take_b[m] = r_next * not_last
    recv_row = recv_ref[...].astype(F32)
    rsum[...] = onehot(iota((buses, slots), 0).astype(F32) == recv_row)
    rback[...] = onehot(iota((slots, buses), 1).astype(F32) == to_column(recv_row))
    link0_row, link1_row = link_ref[0:1, :].astype(F32), link_ref[1:2, :].astype(F32)
    link0, link1 = to_column(link0_row), to_column(link1_row)

    def incidence(d):
        index = (iota((links, buses), 1) + d * buses).astype(F32)
        return jnp.where(index == link0, 1.0, 0.0) - jnp.where(index == link1, 1.0, 0.0)

    ct[...] = incidence(dev).astype(BF16)
    index = (iota((buses, links), 0) + dev * buses).astype(F32)
    cm[...] = (
        jnp.where(index == link0_row, 1.0, 0.0) - jnp.where(index == link1_row, 1.0, 0.0)
    ).astype(BF16)
    for ij in range(9):
        zcol[ij] = jnp.broadcast_to(to_column(imp_ref[ij // 3, ij % 3 : ij % 3 + 1, :]), (buses, cases))

    def advance():
        for m in range(3):
            f, b = fwd[m], bwd[m]
            fwd[m] = keep_f[m] * pltpu.roll(f, 1, 0) + take_f[m] * b
            bwd[m] = keep_b[m] * pltpu.roll(b, segs - 1, 0) + take_b[m] * f

    wait(imp_all, devs - 1, imp_sem.at[1])
    minv[...] = jnp.zeros_like(minv)
    eye = iota((links, links), 0) == iota((links, links), 1)

    @pl.loop(0, devs)
    def _(d):
        c = incidence(d)
        for i in range(3):
            for j in range(i + 1):
                z = imp_all[d, i, j : j + 1, :]
                minv[i * links : (i + 1) * links, j * links : (j + 1) * links] += lax.dot_general(
                    c * z, c, (((1,), (1,)), ((), ())), precision=EXACT, preferred_element_type=F32
                )

    for i in range(3):
        span = slice(i * links, (i + 1) * links)
        minv[span, span] += jnp.where(eye, resist_ref[...], 0.0)
        for j in range(i):
            past = slice(j * links, (j + 1) * links)
            minv[past, span] = minv[span, past]
    order = 3 * links
    lane = iota((order, order), 1)

    @pl.loop(0, links)
    def _(n):
        spots = [n + u * links for u in range(3)]
        a = minv[...]
        rows = [minv[pl.ds(k, 1), :] for k in spots]
        here = [lane == k for k in spots]
        edge = [lane[:1] == k for k in spots]
        cols = [jnp.sum(jnp.where(h, a, 0.0), axis=1, keepdims=True) for h in here]
        block = [
            [jnp.sum(jnp.where(g, r, 0.0), axis=1, keepdims=True) for g in edge] for r in rows
        ]
        for v in range(3):
            inverse = 1.0 / block[v][v]
            row, col = rows[v], cols[v] * inverse
            a = a - col * row
            scaled = row * inverse
            factor = [block[u][v] for u in range(3)]
            across = [block[v][w] * inverse for w in range(3)]
            for u in range(3):
                rows[u] = scaled if u == v else rows[u] - factor[u] * scaled
                cols[u] = col if u == v else cols[u] - block[v][u] * col
            for u in range(3):
                for w in range(3):
                    if u != v and w != v:
                        block[u][w] = block[u][w] - factor[u] * across[w]
            for u in range(3):
                if u != v:
                    block[u][v], block[v][u] = factor[u] * inverse, across[u]
            block[v][v] = -inverse
        for u in range(3):
            a = jnp.where(here[u], cols[u], a)
            for w in range(3):
                rows[u] = jnp.where(edge[w], block[u][w], rows[u])
        minv[...] = a
        for u in range(3):
            minv[pl.ds(spots[u], 1), :] = rows[u]

    def apply(step, values):
        return [
            zcol[3 * i] * values[0] + zcol[3 * i + 1] * values[1] + zcol[3 * i + 2] * values[2]
            for i in range(3)
        ]

    def finish(step):
        advance()
        wait(h_recv.at[step], total - 1, recv_sem.at[0, step])
        for i in range(3):
            part = h_recv[step, :, :, i * cases : (i + 1) * cases].reshape(slots, cases)
            inj[i] = src_ref[step, i] + pick(rsum[...], part)
        open_volts = apply(step, [inj[i] for i in range(3)])
        for i in range(3):
            e_send[step, :, :, i * cases : (i + 1) * cases] = pick(
                ct[...], open_volts[i]
            ).reshape(owners, 8, cases)
        push_shares(step)

        @pl.when(dev < owners)
        def _():
            sum_shares(step)
            wait(g_recv.at[step], owners - 1, recv_sem.at[2, step])

        @pl.when(dev >= owners)
        def _():
            wait(g_recv.at[step], owners, recv_sem.at[2, step])

        stacked = jnp.concatenate(
            [
                g_recv[step, :, :, i * cases : (i + 1) * cases].reshape(links, cases)
                for i in range(3)
            ],
            axis=0,
        )
        current = jnp.dot(minv[...], stacked, precision=EXACT, preferred_element_type=F32)
        net = [
            inj[i] + pick(cm[...], current[i * links : (i + 1) * links]) for i in range(3)
        ]
        volts = apply(step, net)
        for i in range(3):
            volt_ref[step, i] = volts[i]
            v_send[step, :, :, i * cases : (i + 1) * cases] = pick(rback[...], volts[i]).reshape(
                total, cap, cases
            )
        push_all(v_send, v_recv, 3, step)
        v_recv[step, me] = v_send[step, me]
        wait(v_recv.at[step], total - 1, recv_sem.at[3, step])
        ends = [
            v_recv[step, :, :, i * cases : (i + 1) * cases].reshape(slots, cases) for i in range(3)
        ]
        for m in range(3):
            out = trans_ref[m, 0] * ends[0] + trans_ref[m, 1] * ends[1] + trans_ref[m, 2] * ends[2]
            out = out - arr[m]
            fwd[m] += pick(gbt[...], out)
            bwd[m] += pick(gft[...], out)

    finish(0)

    @pl.loop(1, STEPS)
    def _(step):
        gather_send(step)
        finish(step)

    wait(imp_all, devs - 1, imp_sem.at[0])

    @pl.loop(0, STEPS)
    def _(step):
        wait(h_send.at[step], total - 1, send_sem.at[0, step])

        @pl.when(dev < owners)
        def _():
            wait(e_send.at[step], owners - 1, send_sem.at[1, step])
            wait(e_recv.at[step], devs - 1, send_sem.at[2, step])

        @pl.when(dev >= owners)
        def _():
            wait(e_send.at[step], owners, send_sem.at[1, step])

        wait(v_send.at[step], total - 1, send_sem.at[3, step])


def on_device(
    areas,
    devs,
    wave_fwd,
    wave_bwd,
    seg_reflect,
    seg_count,
    modal_admit,
    modal_transform,
    end_slot,
    recv_bus,
    bus_impedance,
    link_bus,
    link_resist,
    source_current,
):
    total = areas * devs
    cases, segs = wave_fwd.shape[2], wave_fwd.shape[1]
    cap = recv_bus.shape[1] // total
    rows = -(-cap // 8) * 8
    if rows != cap:
        end_slot = end_slot // cap * rows + end_slot % cap
        recv_bus = jnp.pad(
            recv_bus.reshape(total, cap), ((0, 0), (0, rows - cap)), constant_values=-1
        ).reshape(1, total * rows)
    slots = total * rows
    buses = bus_impedance.shape[2]
    links = link_bus.shape[0]
    vmem = pl.BlockSpec(memory_space=pltpu.VMEM)
    smem = pl.BlockSpec(memory_space=pltpu.SMEM)
    wide = 3 * cases
    volts, fwd, bwd = pl.pallas_call(
        functools.partial(kernel, areas, devs),
        out_shape=(
            jax.ShapeDtypeStruct((STEPS, 3, buses, cases), F32),
            jax.ShapeDtypeStruct(wave_fwd.shape, F32),
            jax.ShapeDtypeStruct(wave_bwd.shape, F32),
        ),
        in_specs=[vmem] * 5 + [smem] + [vmem] * 6,
        out_specs=(vmem, vmem, vmem),
        scratch_shapes=[
            pltpu.VMEM((STEPS, total, rows, wide), F32),
            pltpu.VMEM((STEPS, total, rows, wide), F32),
            pltpu.VMEM((STEPS, links // 8, 8, wide), F32),
            pltpu.VMEM((STEPS, devs, 8, wide), F32),
            pltpu.VMEM((STEPS, links // 8, 8, wide), F32),
            pltpu.VMEM((STEPS, total, rows, wide), F32),
            pltpu.VMEM((STEPS, total, rows, wide), F32),
            pltpu.VMEM((devs, 3, 3, buses), F32),
            pltpu.VMEM((slots, segs), BF16),
            pltpu.VMEM((slots, segs), BF16),
            pltpu.VMEM((segs, slots), BF16),
            pltpu.VMEM((segs, slots), BF16),
            pltpu.VMEM((buses, slots), BF16),
            pltpu.VMEM((slots, buses), BF16),
            pltpu.VMEM((links, buses), BF16),
            pltpu.VMEM((buses, links), BF16),
            pltpu.VMEM((3, slots, cases), F32),
            pltpu.VMEM((9, buses, cases), F32),
            pltpu.VMEM((3, segs, cases), F32),
            pltpu.VMEM((3, segs, cases), F32),
            pltpu.VMEM((3, segs, cases), F32),
            pltpu.VMEM((3, segs, cases), F32),
            pltpu.VMEM((3, slots, cases), F32),
            pltpu.VMEM((3, buses, cases), F32),
            pltpu.VMEM((3 * links, 3 * links), F32),
            pltpu.SemaphoreType.DMA((4, STEPS)),
            pltpu.SemaphoreType.DMA((4, STEPS)),
            pltpu.SemaphoreType.DMA((2,)),
        ],
        compiler_params=pltpu.CompilerParams(
            collective_id=0, has_side_effects=True, vmem_limit_bytes=60 * 1024 * 1024
        ),
        name="transient",
    )(
        wave_fwd,
        wave_bwd,
        seg_reflect,
        seg_count,
        modal_admit,
        modal_transform,
        end_slot.T,
        recv_bus,
        bus_impedance,
        link_bus.T,
        link_resist.reshape(1, links),
        jnp.transpose(source_current, (0, 2, 1, 3)),
    )
    return (jnp.transpose(volts, (0, 2, 1, 3)), fwd, bwd)


def solution(mesh):
    in_specs = (
        P(None, ("area", "dev"), None),
        P(None, ("area", "dev"), None),
        P(None, ("area", "dev")),
        P(("area", "dev"), None),
        P(None, ("area", "dev")),
        P(),
        P(("area", "dev"), None),
        P(("area", "dev"), None),
        P(None, None, ("area", "dev")),
        P("area", None),
        P("area"),
        P(None, ("area", "dev"), None, None),
    )
    out_specs = (
        P(None, ("area", "dev"), None, None),
        P(None, ("area", "dev"), None),
        P(None, ("area", "dev"), None),
    )
    return jax.shard_map(
        functools.partial(on_device, mesh.shape["area"], mesh.shape["dev"]),
        mesh=mesh,
        in_specs=in_specs,
        out_specs=out_specs,
        check_vma=False,
    )
```
